32 devices in a mesh: tp: 4 (over x, core), ad: 8 (over z, y).
Axes of the slice: x: 2, y: 2, z: 4, core: 2. Of those that a mesh axis runs over, the one named last changes fastest.
Arguments:
- hidden: bfloat16 [3584, 8192], P('ad'), may hold values from -6 to 6
- gain: bfloat16 [8192], replicated, may hold values from 0.25 to 1.75
- key_value_weight: bfloat16 [8192, 2, 1024], P(None, None, 'tp'), may hold values from -0.0625 to 0.0625
- adapter_down_weight: bfloat16 [16, 8192, 128], P('ad', 'tp'), may hold values from -0.0625 to 0.0625
- adapter_up_weight: bfloat16 [16, 2, 64, 1024], P('ad', None, None, 'tp'), may hold values from -0.75 to 0.75
- language_pair_index: int32 [3584], P('ad'), may hold values from 0 to 15, as said below
- adapter_row_index: int32 [16], replicated, may hold values from 0 to 15, as said below
Outputs:
- kv_out: bfloat16 [3584, 2, 1024], P('ad', None, 'tp')
The draws below stay inside these ranges and needn't reach their ends.
Inputs may be any that keep to these rules, and one draw needn't show every extreme that they name: A row's owner is adapter_row_index[language_pair_index] // 2. Among the rows of one device, one owner, the same for every device, has exactly 224 rows; every other owner has at most 112, and one other owner, the same for every device, exactly 112. `adapter_row_index`: each adapter's row in adapter_down_weight and adapter_up_weight; every row appears once.
All inputs are finite; a program needn't handle non-finite values.
Results may differ from the reference program's by a relative error of at most 0.0053.
Values may be sent and summed in bfloat16 or wider, within the bound.
A program may use at most 128 MiB of HBM per device.

```python
import jax
import jax.numpy as jnp
from jax import lax

MODEL_DIM = 8192
KEY_VALUE_WIDTH = 1024
ADAPTER_RANK = 64
ADAPT_DEV = 2
TOK_DEV = 448
ADAPTER_COUNT = 16
ROWS = 3584
CAP_ALL = 224
CAP_REST = 112
N_AD = 8


def plan_tables(key):
    slot_of = jax.random.permutation(jax.random.fold_in(key, 11), ADAPTER_COUNT).astype(jnp.int32)
    adapter_at = jnp.argsort(slot_of, stable=True).astype(jnp.int32)
    hot_owner = jax.random.randint(jax.random.fold_in(key, 12), (), 0, N_AD, dtype=jnp.int32)
    step_up = jax.random.randint(jax.random.fold_in(key, 13), (), 1, N_AD, dtype=jnp.int32)
    second = (hot_owner + step_up) % N_AD
    rank_of = jax.random.permutation(jax.random.fold_in(key, 14), N_AD).astype(jnp.int32)
    weight_of = 1 + 7 * rank_of // (N_AD - 1)
    cand_count = N_AD * CAP_REST

    def one_block(block_index):
        block_key = jax.random.fold_in(key, 1000 + block_index)
        candidates = jnp.repeat(jnp.arange(N_AD, dtype=jnp.int32), CAP_REST)
        usable = (candidates != hot_owner) & (candidates != second)
        positions = jnp.arange(cand_count, dtype=jnp.int32)
        random_draw = jax.random.randint(jax.random.fold_in(block_key, 1), (cand_count,), 0, 4096, dtype=jnp.int32)
        scores = random_draw * weight_of[candidates] * cand_count + positions
        scores = jnp.where(usable, scores, -1 - positions)
        picked = lax.top_k(scores, TOK_DEV - CAP_ALL - CAP_REST)[1]
        owners = jnp.concatenate([jnp.full((CAP_ALL,), hot_owner, jnp.int32), jnp.full((CAP_REST,), second, jnp.int32), candidates[picked]])
        within = jax.random.randint(jax.random.fold_in(block_key, 2), (TOK_DEV,), 0, ADAPT_DEV, dtype=jnp.int32)
        block_pairs = adapter_at[owners * ADAPT_DEV + within]
        shuffle = jax.random.permutation(jax.random.fold_in(block_key, 3), TOK_DEV)
        return block_pairs[shuffle]
    all_pairs = jax.vmap(one_block)(jnp.arange(N_AD, dtype=jnp.int32)).reshape(ROWS).astype(jnp.int32)
    return (slot_of, all_pairs)


def draw_language_pair_index(key, part):
    return plan_tables(key)[1]


def draw_adapter_row_index(key, part):
    return plan_tables(key)[0]


def block_scale(key, extent, pieces, low, top_value):
    level = 1.0
    for position, shards_of in pieces:
        draws = jax.random.uniform(jax.random.fold_in(jax.random.fold_in(key, 6), position), (shards_of,), jnp.float32, low / len(pieces), top_value / len(pieces))
        level = level * jnp.repeat(jnp.exp(draws), extent[position] // shards_of).reshape((-1,) + (1,) * (len(extent) - 1 - position))
    return level


def gaussian(stream_key, shape, scale, most, pieces=(), kind=jnp.bfloat16):
    entries = jax.random.normal(stream_key, shape, jnp.float32) * scale
    if len(pieces) > 0:
        entries = block_scale(stream_key, shape, pieces, -0.22, 0.18) * entries
    return jnp.clip(entries, min=-most, max=most).astype(kind)


def setup_inputs(seed: int = 0) -> dict:
    key_of = jax.random.split(jax.random.key(seed), 8)
    return {
        "hidden": gaussian(key_of[0], (ROWS, MODEL_DIM), 1.0, 6.0, ((0, 8),)),
        "gain": jnp.clip(1.0 + 0.15 * jax.random.normal(key_of[1], (MODEL_DIM,), jnp.float32), 0.25, 1.75).astype(jnp.bfloat16),
        "key_value_weight": gaussian(key_of[2], (MODEL_DIM, 2, KEY_VALUE_WIDTH), MODEL_DIM ** -0.5, 0.0625, ((2, 4),)),
        "adapter_down_weight": gaussian(key_of[3], (ADAPTER_COUNT, MODEL_DIM, 2 * ADAPTER_RANK), MODEL_DIM ** -0.5, 0.0625, ((0, 8), (1, 4))),
        "adapter_up_weight": gaussian(key_of[4], (ADAPTER_COUNT, 2, ADAPTER_RANK, KEY_VALUE_WIDTH), ADAPTER_RANK ** -0.5, 0.75, ((0, 8), (3, 4))),
        "language_pair_index": draw_language_pair_index(jax.random.fold_in(key_of[7], 71), 0),
        "adapter_row_index": draw_adapter_row_index(jax.random.fold_in(key_of[7], 71), 0),
    }


epsilon = 1e-05
adapter_scale = 0.5

def reference(hidden, gain, key_value_weight, adapter_down_weight, adapter_up_weight, language_pair_index, adapter_row_index):
    wide_hidden = hidden.astype(jnp.float32)
    inv_rms = lax.rsqrt(lax.optimization_barrier(jnp.mean(wide_hidden * wide_hidden, axis=-1, keepdims=True)) + epsilon)
    normed = (wide_hidden * inv_rms * gain.astype(jnp.float32)).astype(jnp.bfloat16)
    base_projection = jnp.dot(normed, key_value_weight.reshape(MODEL_DIM, 2 * KEY_VALUE_WIDTH), preferred_element_type=jnp.float32).reshape(ROWS, 2, KEY_VALUE_WIDTH)
    slot_ids = adapter_row_index[language_pair_index].astype(jnp.int32)
    sorting_order = jnp.argsort(slot_ids, stable=True).astype(jnp.int32)
    sorted_slots = slot_ids[sorting_order]
    labels = jnp.arange(ADAPTER_COUNT, dtype=jnp.int32)
    counts = lax.optimization_barrier(jnp.sum((sorted_slots[None, :] == labels[:, None]).astype(jnp.int32), axis=1))
    starts = (jnp.cumsum(counts) - counts).astype(jnp.int32)
    longest = CAP_ALL * N_AD
    padded = jnp.concatenate([normed[sorting_order], jnp.zeros((longest, MODEL_DIM), jnp.bfloat16)], 0)
    padded_slots = jnp.concatenate([sorted_slots, jnp.full((longest,), -1, jnp.int32)], 0)

    def add_adapter(adapter_entry, totals):
        adapter_entry = jnp.asarray(adapter_entry).astype(jnp.int32)
        begin_row = starts[adapter_entry].astype(jnp.int32)
        block_row_count = lax.dynamic_slice_in_dim(padded, begin_row, longest, 0)
        block_slots = lax.dynamic_slice_in_dim(padded_slots, begin_row, longest, 0)
        reduced_rank_state = jnp.dot(block_row_count, adapter_down_weight[adapter_entry], preferred_element_type=jnp.float32).astype(jnp.bfloat16)
        key_portion = jnp.dot(reduced_rank_state[:, :ADAPTER_RANK], adapter_up_weight[adapter_entry, 0], preferred_element_type=jnp.float32)
        value_portion = jnp.dot(reduced_rank_state[:, ADAPTER_RANK:], adapter_up_weight[adapter_entry, 1], preferred_element_type=jnp.float32)
        narrow = jnp.stack([key_portion, value_portion], 1).astype(jnp.bfloat16)
        narrow = lax.optimization_barrier(narrow)
        delta_block = narrow.astype(jnp.float32)
        keep_mask = (block_slots == adapter_entry)[:, None, None]
        current = lax.dynamic_slice_in_dim(totals, begin_row, longest, 0)
        update = current + jnp.where(keep_mask, delta_block, jnp.float32(0.0))
        return lax.dynamic_update_slice_in_dim(totals, update, begin_row, 0)
    totals = lax.fori_loop(0, ADAPTER_COUNT, add_adapter, jnp.zeros((ROWS + longest, 2, KEY_VALUE_WIDTH), jnp.float32))
    delta_sorted = totals[:ROWS]
    delta_complete = jnp.zeros_like(delta_sorted).at[sorting_order].set(delta_sorted)
    return (base_projection + adapter_scale * delta_complete).astype(jnp.bfloat16)
```

```python
import jax
import jax.numpy as jnp
from jax import lax
from jax.sharding import PartitionSpec as P

epsilon = 1e-05
adapter_scale = 0.5


def ring_order(count):
    return list(range(0, count, 2)) + list(reversed(range(1, count, 2)))


def on_device(
    hidden,
    gain,
    key_value_weight,
    adapter_down_weight,
    adapter_up_weight,
    language_pair_index,
    adapter_row_index,
):
    tok_count, model_width = hidden.shape
    owners = lax.axis_size("ad")
    held, column_portion, low_width = adapter_down_weight.shape
    head_cols = key_value_weight.shape[2]
    rank = adapter_up_weight.shape[2]
    me = lax.axis_index("ad")

    order = ring_order(owners)
    forward = [(order[i], order[(i + 1) % owners]) for i in range(owners)]
    backward = [(b, a) for a, b in forward]
    place = [order.index(i) for i in range(owners)]
    my_place = jnp.asarray(place, jnp.int32)[me]
    order_table = jnp.asarray(order, jnp.int32)

    up_all = lax.all_gather(adapter_up_weight, "ad", axis=0, tiled=True)

    wide_hidden = hidden.astype(jnp.float32)
    inv_rms = lax.rsqrt(jnp.mean(wide_hidden * wide_hidden, axis=-1, keepdims=True) + epsilon)
    normed = (wide_hidden * inv_rms * gain.astype(jnp.float32)).astype(jnp.bfloat16)
    own_cols = lax.dynamic_slice_in_dim(
        normed, lax.axis_index("tp") * column_portion, column_portion, 1
    )
    slot_ids = adapter_row_index[language_pair_index]

    def term(block, first_id):
        total = jnp.zeros((tok_count, low_width), jnp.float32)
        for j in range(block.shape[0]):
            low = jnp.dot(own_cols, block[j], preferred_element_type=jnp.float32)
            total = total + jnp.where((slot_ids == first_id + j)[:, None], low, jnp.float32(0.0))
        return total

    low = term(adapter_down_weight, me * held)
    up_block = down_block = adapter_down_weight
    half = held // 2
    for step in range(1, owners // 2 + 1):
        from_behind = order_table[lax.rem(my_place + owners - step, owners)]
        from_ahead = order_table[lax.rem(my_place + step, owners)]
        if step < owners // 2:
            up_block = lax.ppermute(up_block, "ad", forward)
            down_block = lax.ppermute(down_block, "ad", backward)
            low = low + term(up_block, from_behind * held) + term(down_block, from_ahead * held)
        else:
            first = lax.ppermute(up_block[:half], "ad", forward)
            rest = lax.ppermute(down_block[half:], "ad", backward)
            low = low + term(first, from_behind * held) + term(rest, from_ahead * held + half)

    low_rank = lax.psum(low, "tp").astype(jnp.bfloat16)
    base = jnp.dot(
        normed,
        key_value_weight.reshape(model_width, 2 * head_cols),
        preferred_element_type=jnp.float32,
    ).reshape(tok_count, 2, head_cols)

    adapters = up_all.shape[0]
    mask = slot_ids[:, None] == jnp.arange(adapters, dtype=jnp.int32)[None, :]
    halves = []
    for c in range(2):
        part = low_rank[:, c * rank : (c + 1) * rank]
        wide = jnp.where(mask[:, :, None], part[:, None, :], jnp.zeros((), jnp.bfloat16))
        halves.append(
            jnp.dot(
                wide.reshape(tok_count, adapters * rank),
                up_all[:, c].reshape(adapters * rank, head_cols),
                preferred_element_type=jnp.float32,
            )
        )
    delta = jnp.stack(halves, axis=1).astype(jnp.bfloat16)
    return (base + adapter_scale * delta.astype(jnp.float32)).astype(jnp.bfloat16)


def solution(mesh):
    return jax.shard_map(
        on_device,
        mesh=mesh,
        in_specs=(
            P("ad", None),
            P(),
            P(None, None, "tp"),
            P("ad", "tp", None),
            P("ad", None, None, "tp"),
            P("ad"),
            P(),
        ),
        out_specs=P("ad", None, "tp"),
        check_vma=False,
    )
```

```python
import jax
import jax.numpy as jnp
from jax import lax
from jax.sharding import PartitionSpec as P

epsilon = 1e-05
adapter_scale = 0.5


def ring_order(count):
    return list(range(0, count, 2)) + list(reversed(range(1, count, 2)))


def tie(*values):
    return lax.optimization_barrier(values)


def base_of(normed, *parts):
    return [jnp.dot(normed, part, preferred_element_type=jnp.float32) for part in parts]


def on_device(
    hidden,
    gain,
    key_value_weight,
    adapter_down_weight,
    adapter_up_weight,
    language_pair_index,
    adapter_row_index,
):
    tok_count, model_width = hidden.shape
    owners = lax.axis_size("ad")
    held, column_portion, low_width = adapter_down_weight.shape
    head_cols = key_value_weight.shape[2]
    rank = adapter_up_weight.shape[2]
    me = lax.axis_index("ad")

    order = ring_order(owners)
    forward = [(order[i], order[(i + 1) % owners]) for i in range(owners)]
    backward = [(b, a) for a, b in forward]
    place = [order.index(i) for i in range(owners)]
    my_place = jnp.asarray(place, jnp.int32)[me]
    order_table = jnp.asarray(order, jnp.int32)

    up_all = lax.all_gather(adapter_up_weight, "ad", axis=0, tiled=True)

    pairs = jnp.arange(adapter_row_index.shape[0], dtype=jnp.int32)
    is_pair = language_pair_index[:, None] == pairs[None, :]
    slot_ids = jnp.sum(jnp.where(is_pair, adapter_row_index[None, :], 0), axis=1, keepdims=True)

    wide_hidden = hidden.astype(jnp.float32)
    inv_rms = lax.rsqrt(jnp.mean(wide_hidden * wide_hidden, axis=-1, keepdims=True) + epsilon)
    normed = (wide_hidden * inv_rms * gain.astype(jnp.float32)).astype(jnp.bfloat16)
    own_cols = lax.dynamic_slice_in_dim(
        normed, lax.axis_index("tp") * column_portion, column_portion, 1
    )
    own_cols, normed, slot_ids = tie(own_cols, normed, slot_ids)

    def term(block, first_id):
        total = jnp.float32(0.0)
        for j in range(block.shape[0]):
            low = jnp.dot(own_cols, block[j], preferred_element_type=jnp.float32)
            total = total + jnp.where(slot_ids == first_id + j, low, jnp.float32(0.0))
        return total

    steps = owners // 2
    half = held // 2
    up_block = down_block = adapter_down_weight
    low = term(adapter_down_weight, me * held)
    waiting = []
    for step in range(1, steps + 1):
        from_behind = order_table[lax.rem(my_place + owners - step, owners)]
        from_ahead = order_table[lax.rem(my_place + step, owners)]
        if step == steps:
            up_block, down_block = up_block[:half], down_block[half:]
        up_next = lax.ppermute(up_block, "ad", forward)
        down_next = lax.ppermute(down_block, "ad", backward)
        if step == 2:
            key_value_weight, up_block, down_block = tie(key_value_weight, up_block, down_block)
            key_part, value_part = tie(key_value_weight[:, 0], key_value_weight[:, 1])
        if step == 3:
            key_part, value_part, up_block, down_block = tie(
                key_part, value_part, up_block, down_block
            )
            base = base_of(normed, key_part, value_part)
        if step >= 3:
            for block, owner in waiting:
                low = low + term(block, owner * held)
            waiting = []
        if step < steps:
            if step == 1:
                up_next, down_next, low = tie(up_next, down_next, low)
            elif step == 2:
                up_next, down_next, key_part, value_part = tie(
                    up_next, down_next, key_part, value_part
                )
            elif step == 3:
                up_next, down_next, low, *base = tie(up_next, down_next, low, *base)
            else:
                up_next, down_next, low = tie(up_next, down_next, low)
            waiting += [(up_next, from_behind), (down_next, from_ahead)]
        else:
            low = low + term(up_next, from_behind * held)
            low = low + term(down_next, from_ahead * held + half)
        up_block, down_block = up_next, down_next

    low_rank = lax.psum(low, "tp").astype(jnp.bfloat16)

    adapters = up_all.shape[0]
    mask = slot_ids == jnp.arange(adapters, dtype=jnp.int32)[None, :]
    halves = []
    for c in range(2):
        part = low_rank[:, c * rank : (c + 1) * rank]
        wide = jnp.where(mask[:, :, None], part[:, None, :], jnp.zeros((), jnp.bfloat16))
        halves.append(
            jnp.dot(
                wide.reshape(tok_count, adapters * rank),
                up_all[:, c].reshape(adapters * rank, head_cols),
                preferred_element_type=jnp.float32,
            )
        )
    outs = [
        (part + adapter_scale * delta.astype(jnp.bfloat16).astype(jnp.float32)).astype(jnp.bfloat16)
        for part, delta in zip(base, halves)
    ]
    return jnp.stack(outs, axis=1)


def solution(mesh):
    return jax.shard_map(
        on_device,
        mesh=mesh,
        in_specs=(
            P("ad", None),
            P(),
            P(None, None, "tp"),
            P("ad", "tp", None),
            P("ad", None, None, "tp"),
            P("ad"),
            P(),
        ),
        out_specs=P("ad", None, "tp"),
        check_vma=False,
    )
```

```python
import jax
import jax.numpy as jnp
from jax import lax
from jax.sharding import PartitionSpec as P

epsilon = 1e-05
adapter_scale = 0.5
UP_LAG = 0


def ring_order(count):
    return list(range(0, count, 2)) + list(reversed(range(1, count, 2)))


def tie(*values):
    return lax.optimization_barrier(values)


def sum_parts(total):
    count = lax.axis_size("tp")
    if count & (count - 1):
        return lax.psum(total, "tp")
    bit = 1
    while bit < count:
        pairs = [(i, i ^ bit) for i in range(count)]
        total = total + lax.ppermute(total.astype(jnp.bfloat16), "tp", pairs).astype(jnp.float32)
        bit *= 2
    return total


def base_of(normed, *parts):
    return [jnp.dot(normed, part, preferred_element_type=jnp.float32) for part in parts]


def on_device(
    hidden,
    gain,
    key_value_weight,
    adapter_down_weight,
    adapter_up_weight,
    language_pair_index,
    adapter_row_index,
):
    tok_count, model_width = hidden.shape
    owners = lax.axis_size("ad")
    held, column_portion, low_width = adapter_down_weight.shape
    head_cols = key_value_weight.shape[2]
    rank = adapter_up_weight.shape[2]
    me = lax.axis_index("ad")

    order = ring_order(owners)
    forward = [(order[i], order[(i + 1) % owners]) for i in range(owners)]
    backward = [(b, a) for a, b in forward]
    place = [order.index(i) for i in range(owners)]
    my_place = jnp.asarray(place, jnp.int32)[me]
    order_table = jnp.asarray(order, jnp.int32)

    pairs = jnp.arange(adapter_row_index.shape[0], dtype=jnp.int32)
    is_pair = language_pair_index[:, None] == pairs[None, :]
    slot_ids = jnp.sum(jnp.where(is_pair, adapter_row_index[None, :], 0), axis=1, keepdims=True)

    wide_hidden = hidden.astype(jnp.float32)
    inv_rms = lax.rsqrt(jnp.mean(wide_hidden * wide_hidden, axis=-1, keepdims=True) + epsilon)
    normed = (wide_hidden * inv_rms * gain.astype(jnp.float32)).astype(jnp.bfloat16)
    own_cols = lax.dynamic_slice_in_dim(
        normed, lax.axis_index("tp") * column_portion, column_portion, 1
    )
    own_cols, normed, slot_ids = tie(own_cols, normed, slot_ids)

    def term(block, first_id):
        total = jnp.float32(0.0)
        for j in range(block.shape[0]):
            low = jnp.dot(own_cols, block[j], preferred_element_type=jnp.float32)
            total = total + jnp.where(slot_ids == first_id + j, low, jnp.float32(0.0))
        return total

    steps = owners // 2
    up_f = up_b = adapter_up_weight
    ups = [adapter_up_weight]
    up_ids = [me * held + jnp.arange(held, dtype=jnp.int32)]
    half = held // 2
    up_block = down_block = adapter_down_weight
    low = term(adapter_down_weight, me * held)
    waiting = []

    def carry_up(step):
        nonlocal up_f, up_b
        behind = order_table[lax.rem(my_place + owners - step, owners)] * held
        ahead = order_table[lax.rem(my_place + step, owners)] * held
        if step == steps:
            up_f, up_b, ahead = up_f[:half], up_b[half:], ahead + half
        up_f = lax.ppermute(up_f, "ad", forward)
        up_b = lax.ppermute(up_b, "ad", backward)
        ups.extend([up_f, up_b])
        up_ids.append(behind + jnp.arange(up_f.shape[0], dtype=jnp.int32))
        up_ids.append(ahead + jnp.arange(up_b.shape[0], dtype=jnp.int32))

    for step in range(1, steps + 1):
        from_behind = order_table[lax.rem(my_place + owners - step, owners)]
        from_ahead = order_table[lax.rem(my_place + step, owners)]
        if step == steps:
            up_block, down_block = up_block[:half], down_block[half:]
        up_next = lax.ppermute(up_block, "ad", forward)
        down_next = lax.ppermute(down_block, "ad", backward)
        if step > UP_LAG:
            carry_up(step - UP_LAG)
        if step == 2:
            key_value_weight, up_block, down_block = tie(key_value_weight, up_block, down_block)
            key_part, value_part = tie(key_value_weight[:, 0], key_value_weight[:, 1])
        if step == 3:
            key_part, value_part, up_block, down_block = tie(
                key_part, value_part, up_block, down_block
            )
            base = base_of(normed, key_part, value_part)
        if step >= 3:
            for block, owner in waiting:
                low = low + term(block, owner * held)
            waiting = []
        if step < steps:
            if step == 1:
                up_next, down_next, low = tie(up_next, down_next, low)
            elif step == 2:
                up_next, down_next, key_part, value_part = tie(
                    up_next, down_next, key_part, value_part
                )
            elif step == 3:
                up_next, down_next, low, *base = tie(up_next, down_next, low, *base)
            else:
                up_next, down_next, low = tie(up_next, down_next, low)
            waiting += [(up_next, from_behind), (down_next, from_ahead)]
        else:
            low = low + term(up_next, from_behind * held)
            low = low + term(down_next, from_ahead * held + half)
        if step < steps:
            up_next, down_next, up_f, up_b = tie(up_next, down_next, up_f, up_b)
        up_block, down_block = up_next, down_next

    for step in range(max(steps - UP_LAG, 0) + 1, steps + 1):
        if step == steps - UP_LAG + 1:
            up_f, up_b, up_block, down_block = tie(up_f, up_b, up_block, down_block)
        carry_up(step)

    low_rank = sum_parts(low).astype(jnp.bfloat16)

    up_all = jnp.concatenate(ups, axis=0)
    adapters = up_all.shape[0]
    mask = slot_ids == jnp.concatenate(up_ids)[None, :]
    halves = []
    for c in range(2):
        part = low_rank[:, c * rank : (c + 1) * rank]
        wide = jnp.where(mask[:, :, None], part[:, None, :], jnp.zeros((), jnp.bfloat16))
        halves.append(
            jnp.dot(
                wide.reshape(tok_count, adapters * rank),
                up_all[:, c].reshape(adapters * rank, head_cols),
                preferred_element_type=jnp.float32,
            )
        )
    outs = [
        (part + adapter_scale * delta.astype(jnp.bfloat16).astype(jnp.float32)).astype(jnp.bfloat16)
        for part, delta in zip(base, halves)
    ]
    return jnp.stack(outs, axis=1)


def solution(mesh):
    return jax.shard_map(
        on_device,
        mesh=mesh,
        in_specs=(
            P("ad", None),
            P(),
            P(None, None, "tp"),
            P("ad", "tp", None),
            P("ad", None, None, "tp"),
            P("ad"),
            P(),
        ),
        out_specs=P("ad", None, "tp"),
        check_vma=False,
    )
```

```python
import jax
import jax.numpy as jnp
from jax import lax
from jax.sharding import PartitionSpec as P

epsilon = 1e-05
adapter_scale = 0.5


def ring_order(count):
    return list(range(0, count, 2)) + list(reversed(range(1, count, 2)))


def tie(*values):
    return lax.optimization_barrier(values)


def sum_parts(total):
    count = lax.axis_size("tp")
    if count & (count - 1):
        return lax.psum(total, "tp")
    bit = 1
    while bit < count:
        pairs = [(i, i ^ bit) for i in range(count)]
        total = total + lax.ppermute(total.astype(jnp.bfloat16), "tp", pairs).astype(jnp.float32)
        bit *= 2
    return total


def base_of(normed, *parts):
    return [jnp.dot(normed, part, preferred_element_type=jnp.float32) for part in parts]


def on_device(
    hidden,
    gain,
    key_value_weight,
    adapter_down_weight,
    adapter_up_weight,
    language_pair_index,
    adapter_row_index,
):
    tok_count, model_width = hidden.shape
    owners = lax.axis_size("ad")
    held, column_portion, low_width = adapter_down_weight.shape
    head_cols = key_value_weight.shape[2]
    rank = adapter_up_weight.shape[2]
    me = lax.axis_index("ad")

    order = ring_order(owners)
    forward = [(order[i], order[(i + 1) % owners]) for i in range(owners)]
    backward = [(b, a) for a, b in forward]
    my_place = jnp.where(me % 2 == 0, me // 2, owners - 1 - me // 2)
    evens = (owners + 1) // 2

    def owner_at(place_of):
        return jnp.where(place_of < evens, 2 * place_of, 2 * (owners - place_of) - 1)

    pairs = jnp.arange(adapter_row_index.shape[0], dtype=jnp.int32)
    is_pair = language_pair_index[:, None] == pairs[None, :]
    slot_ids = jnp.sum(jnp.where(is_pair, adapter_row_index[None, :], 0), axis=1, keepdims=True)

    wide_hidden = hidden.astype(jnp.float32)
    inv_rms = lax.rsqrt(jnp.mean(wide_hidden * wide_hidden, axis=-1, keepdims=True) + epsilon)
    normed = (wide_hidden * inv_rms * gain.astype(jnp.float32)).astype(jnp.bfloat16)
    own_cols = lax.dynamic_slice_in_dim(
        normed, lax.axis_index("tp") * column_portion, column_portion, 1
    )
    own_cols, normed = tie(own_cols, normed)

    def term(block, first_id):
        total = jnp.float32(0.0)
        for j in range(block.shape[0]):
            low = jnp.dot(own_cols, block[j], preferred_element_type=jnp.float32)
            total = total + jnp.where(slot_ids == first_id + j, low, jnp.float32(0.0))
        return total

    steps = owners // 2
    up_f = up_b = adapter_up_weight
    ups = [adapter_up_weight]
    up_ids = [me * held + jnp.arange(held, dtype=jnp.int32)]
    half = held // 2
    up_block = down_block = adapter_down_weight
    low = jnp.zeros((tok_count, low_width), jnp.float32)
    waiting = [(adapter_down_weight, me)]

    def carry_up(step):
        nonlocal up_f, up_b
        behind = owner_at(lax.rem(my_place + owners - step, owners)) * held
        ahead = owner_at(lax.rem(my_place + step, owners)) * held
        if step == steps:
            up_f, up_b, ahead = up_f[:half], up_b[half:], ahead + half
        up_f = lax.ppermute(up_f, "ad", forward)
        up_b = lax.ppermute(up_b, "ad", backward)
        ups.extend([up_f, up_b])
        up_ids.append(behind + jnp.arange(up_f.shape[0], dtype=jnp.int32))
        up_ids.append(ahead + jnp.arange(up_b.shape[0], dtype=jnp.int32))

    for step in range(1, steps + 1):
        from_behind = owner_at(lax.rem(my_place + owners - step, owners))
        from_ahead = owner_at(lax.rem(my_place + step, owners))
        if step == steps:
            up_block, down_block = up_block[:half], down_block[half:]
        up_next = lax.ppermute(up_block, "ad", forward)
        down_next = lax.ppermute(down_block, "ad", backward)
        carry_up(step)
        if step == 2:
            key_value_weight, up_block, down_block = tie(key_value_weight, up_block, down_block)
            key_part, value_part = tie(key_value_weight[:, 0], key_value_weight[:, 1])
        if step == 3:
            key_part, value_part, up_block, down_block = tie(
                key_part, value_part, up_block, down_block
            )
            base = base_of(normed, key_part, value_part)
        if step >= 3:
            for block, owner in waiting:
                low = low + term(block, owner * held)
            waiting = []
        if step < steps:
            if step == 1:
                up_next, down_next, own_cols = tie(up_next, down_next, own_cols)
            elif step == 2:
                up_next, down_next, key_part, value_part = tie(
                    up_next, down_next, key_part, value_part
                )
            elif step == 3:
                up_next, down_next, low, *base = tie(up_next, down_next, low, *base)
            else:
                up_next, down_next, low = tie(up_next, down_next, low)
            waiting += [(up_next, from_behind), (down_next, from_ahead)]
        else:
            low = low + term(up_next, from_behind * held)
            low = low + term(down_next, from_ahead * held + half)
        if step < steps:
            up_next, down_next, up_f, up_b = tie(up_next, down_next, up_f, up_b)
        up_block, down_block = up_next, down_next

    low_rank = sum_parts(low).astype(jnp.bfloat16)

    up_all = jnp.concatenate(ups, axis=0)
    adapters = up_all.shape[0]
    mask = slot_ids == jnp.concatenate(up_ids)[None, :]
    halves = []
    for c in range(2):
        part = low_rank[:, c * rank : (c + 1) * rank]
        wide = jnp.where(mask[:, :, None], part[:, None, :], jnp.zeros((), jnp.bfloat16))
        halves.append(
            jnp.dot(
                wide.reshape(tok_count, adapters * rank),
                up_all[:, c].reshape(adapters * rank, head_cols),
                preferred_element_type=jnp.float32,
            )
        )
    outs = [
        (part + adapter_scale * delta.astype(jnp.bfloat16).astype(jnp.float32)).astype(jnp.bfloat16)
        for part, delta in zip(base, halves)
    ]
    return jnp.stack(outs, axis=1)


def solution(mesh):
    return jax.shard_map(
        on_device,
        mesh=mesh,
        in_specs=(
            P("ad", None),
            P(),
            P(None, None, "tp"),
            P("ad", "tp", None),
            P("ad", None, None, "tp"),
            P("ad"),
            P(),
        ),
        out_specs=P("ad", None, "tp"),
        check_vma=False,
    )
```
